32 devices in a mesh: row: 4 (over x, core), col: 8 (over z, y).
Axes of the slice: x: 2, y: 2, z: 4, core: 2. Of those that a mesh axis runs over, the one named last changes fastest.
Arguments:
- coefficients: float32 [8, 8192, 8192], P(None, 'row', 'col'), may hold values from -40 to 40, as said below
- lambdas: float32 [256], replicated, may hold values from -0.95 to 0.95
- right_vecs: float32 [8192, 256], P(('col', 'row')), may hold values from -6 to 6
- left_vecs: float32 [8192, 256], P(('row', 'col')), may hold values from -6 to 6
Outputs:
- right_resid: float32 [8192, 256], P(('row', 'col'))
- left_resid: float32 [8192, 256], P(('col', 'row'))
- root_mean: float32 [2, 256], replicated
The draws below stay inside these ranges and needn't reach their ends.
Inputs may be any that keep to these rules, and one draw needn't show every extreme that they name: `coefficients`: the entries of every coefficient matrix.
All inputs are finite; a program needn't handle non-finite values.
Results may differ from the reference program's by a relative error of at most 0.0001.
Values sent between devices are 32-bit elements; how exact they have to be, the bound alone decides.
No kernel may reach another device: no remote copies, remote signals or barrier semaphores. Data moves between devices by JAX's collectives and lax.ppermute only.
A program may use at most 128 MiB of HBM per device.

```python
import math
import jax
import jax.numpy as jnp
from jax import lax

N = 8192
K = 8
TRIP = 256


def draw_coefficients(key, part):
    subkeys = jax.random.split(jax.random.fold_in(key, 17), 3)
    positions = jnp.arange(N, dtype=jnp.float32) / N
    trend_scale = 3.0 ** (positions - 0.5)
    low_log = -0.5 * math.log(10.0)
    high_log = 0.5 * math.log(10.0)
    row_scale = trend_scale * jnp.exp(jax.random.uniform(subkeys[0], (N,), jnp.float32, low_log, high_log))
    col_scale = trend_scale * jnp.exp(jax.random.uniform(subkeys[1], (N,), jnp.float32, low_log, high_log))
    random_part = jnp.clip(jax.random.normal(subkeys[2], (K, N, N), jnp.float32), -6.0, 6.0)
    matrices = random_part / math.sqrt(N) * row_scale[None, :, None] * col_scale[None, None, :]
    identity_mask = (jnp.arange(N)[:, None] == jnp.arange(N)[None, :]).astype(jnp.float32)
    matrices = matrices.at[0].add(0.5 * identity_mask * (row_scale * col_scale)[:, None])
    return matrices


def levels(rng, dims, pieces, low, largest):
    def one(axis_at, parts):
        steps = jax.random.uniform(jax.random.fold_in(jax.random.fold_in(rng, 6), axis_at), (parts,), jnp.float32, low / len(pieces), largest / len(pieces))
        return jnp.repeat(jnp.exp(steps), dims[axis_at] // parts).reshape((-1,) + (1,) * (len(dims) - axis_at - 1))

    level = one(*pieces[0])
    for cut in pieces[1:]:
        level = level * one(*cut)
    return level


def scatter_about(stream_key, extent, scale, most, cuts=(), held_as=jnp.bfloat16):
    array = jax.random.normal(stream_key, extent, jnp.float32) * scale
    if len(cuts) > 0:
        array = levels(stream_key, extent, cuts, -0.22, 0.18) * array
    return jnp.clip(array, min=-most, max=most).astype(held_as)


def setup_inputs(seed: int = 0) -> dict:
    splits = jax.random.split(jax.random.key(seed), 5)
    coefficients = draw_coefficients(jax.random.fold_in(splits[4], 71), 0)
    lambdas = jnp.clip(jax.random.uniform(splits[1], (TRIP,), jnp.float32, -0.95, 0.95), -0.95, 0.95)
    right_vecs = scatter_about(splits[2], (N, TRIP), 1.0, 6.0, ((0, 32),), jnp.float32)
    left_vecs = scatter_about(splits[3], (N, TRIP), 1.0, 6.0, ((0, 32),), jnp.float32)
    return dict(coefficients=coefficients, lambdas=lambdas, right_vecs=right_vecs, left_vecs=left_vecs)


epsilon = 1e-06

def chebyshev(lambdas, count):
    terms = [jnp.ones_like(lambdas), lambdas]
    while len(terms) < count:
        terms.append(2.0 * lambdas * terms[-1] - terms[-2])
    return jnp.stack(terms[:count])

def reference(coefficients, lambdas, right_vecs, left_vecs):
    weights = chebyshev(lambdas, K)
    right_sum = jnp.zeros((N, TRIP), jnp.float32)
    left_sum = jnp.zeros((N, TRIP), jnp.float32)
    for term in range(K):
        matrix = coefficients[term]
        right_sum = right_sum + jnp.dot(matrix, right_vecs * weights[term][None, :], precision=lax.Precision.HIGHEST, preferred_element_type=jnp.float32)
        left_sum = left_sum + lax.dot_general(matrix, left_vecs * weights[term][None, :], (((0,), (0,)), ((), ())), precision=lax.Precision.HIGHEST, preferred_element_type=jnp.float32)
    squares = jnp.stack([lax.optimization_barrier(jnp.mean(right_sum * right_sum, axis=0)), lax.optimization_barrier(jnp.mean(left_sum * left_sum, axis=0))])
    return (right_sum, left_sum, jnp.sqrt(squares + epsilon))
```

```python
import functools
import jax
import jax.numpy as jnp
from jax import lax
from jax.experimental import pallas as pl
from jax.experimental.pallas import tpu as pltpu
from jax.sharding import PartitionSpec as P

LANES = 128
SLOTS = 3
VMEM_LIMIT = 48 * 2**20

epsilon = 1e-06


def chebyshev(lambdas, count):
    terms = [jnp.ones_like(lambdas), lambdas]
    while len(terms) < count:
        terms.append(2.0 * lambdas * terms[-1] - terms[-2])
    return jnp.stack(terms[:count])


def ring_order(count):
    return list(range(0, count, 2)) + list(range(1, count, 2))[::-1]


def halves(values):
    high = values.astype(jnp.bfloat16)
    return high, (values - high.astype(jnp.float32)).astype(jnp.bfloat16)


def product(left, right, dims):
    def dot(a, b):
        return lax.dot_general(a, b, (dims, ((), ())), preferred_element_type=jnp.float32)

    (left_high, left_low), (right_high, right_low) = left, right
    return dot(left_high, right_high) + dot(left_high, right_low) + dot(left_low, right_high)


def block_copies(matrices_ref, place, buffer, sem):
    width = buffer.shape[2]
    columns = pl.ds(pl.multiple_of(place * width, width), width)

    def copy(term):
        slot = lax.rem(term, SLOTS)
        return pltpu.make_async_copy(matrices_ref.at[term, :, columns], buffer.at[slot], sem.at[slot])

    return copy


def each_matrix(count, copy, step):
    def visit(term, carry):
        copy(term).wait()
        ahead = term + SLOTS - 1

        @pl.when((term > 0) & (ahead < count))
        def _():
            copy(ahead).start()

        step(term)
        return carry

    lax.fori_loop(0, count, visit, 0)


def right_kernel(order, has_total, place_ref, matrices_ref, vecs_ref, weights_ref, *rest):
    total_ref = rest[0] if has_total else None
    out_ref, high, low, buffer, sem, total_sem = rest[-6:]
    count, rows, _ = matrices_ref.shape
    chunk = rows // len(order)
    copy = block_copies(matrices_ref, place_ref[0], buffer, sem)
    for term in range(min(SLOTS, count)):
        copy(jnp.int32(term)).start()
    if has_total:
        fetch = pltpu.make_async_copy(total_ref, out_ref, total_sem)
        fetch.start()
    else:
        out_ref[...] = jnp.zeros_like(out_ref)

    def weigh(term, carry):
        high[term], low[term] = halves(vecs_ref[...] * weights_ref[pl.ds(term, 1), :])
        return carry

    lax.fori_loop(0, count, weigh, 0)
    if has_total:
        fetch.wait()

    def step(term):
        terms = product(halves(buffer[lax.rem(term, SLOTS)]), (high[term], low[term]), ((1,), (0,)))
        for at, member in enumerate(order):
            out_ref[at * chunk : (at + 1) * chunk, :] += terms[member * chunk : (member + 1) * chunk, :]

    each_matrix(count, copy, step)


def left_kernel(order, place_ref, matrices_ref, vecs_ref, weights_ref, out_ref, buffer, sem):
    count, rows, _ = matrices_ref.shape
    chunk = rows // len(order)
    copy = block_copies(matrices_ref, place_ref[0], buffer, sem)
    for term in range(min(SLOTS, count)):
        copy(jnp.int32(term)).start()
    out_ref[...] = jnp.zeros_like(out_ref)
    at = [order.index(member) for member in range(len(order))]

    def step(term):
        vecs = jnp.concatenate([vecs_ref[i * chunk : (i + 1) * chunk, :] for i in at], axis=0)
        weighted = halves(vecs * weights_ref[pl.ds(term, 1), :])
        out_ref[...] += product(halves(buffer[lax.rem(term, SLOTS)]), weighted, ((0,), (0,)))

    each_matrix(count, copy, step)


VMEM = pl.BlockSpec(memory_space=pltpu.VMEM)
SMEM = pl.BlockSpec(memory_space=pltpu.SMEM)
ANY = pl.BlockSpec(memory_space=pl.ANY)


def cost(count, rows, width, trip):
    return pl.CostEstimate(
        flops=6 * count * rows * width * trip, bytes_accessed=4 * count * rows * width, transcendentals=0
    )


def right_terms(order, matrices, vecs, weights, place, total=None):
    count, rows, _ = matrices.shape
    width, trip = vecs.shape
    return pl.pallas_call(
        functools.partial(right_kernel, order, total is not None),
        out_shape=jax.ShapeDtypeStruct((rows, trip), jnp.float32),
        in_specs=[SMEM, ANY, VMEM, VMEM] + ([ANY] if total is not None else []),
        out_specs=VMEM,
        scratch_shapes=[
            pltpu.VMEM((count, width, trip), jnp.bfloat16),
            pltpu.VMEM((count, width, trip), jnp.bfloat16),
            pltpu.VMEM((SLOTS, rows, width), jnp.float32),
            pltpu.SemaphoreType.DMA((SLOTS,)),
            pltpu.SemaphoreType.DMA,
        ],
        compiler_params=pltpu.CompilerParams(vmem_limit_bytes=VMEM_LIMIT),
        cost_estimate=cost(count, rows, width, trip),
        name="right_terms",
    )(jnp.reshape(place, (1,)), matrices, vecs, weights, *([total] if total is not None else []))


def left_terms(order, matrices, vecs, weights, place, width):
    count, rows, _ = matrices.shape
    trip = vecs.shape[1]
    return pl.pallas_call(
        functools.partial(left_kernel, order),
        out_shape=jax.ShapeDtypeStruct((width, trip), jnp.float32),
        in_specs=[SMEM, ANY, VMEM, VMEM],
        out_specs=VMEM,
        scratch_shapes=[
            pltpu.VMEM((SLOTS, rows, width), jnp.float32),
            pltpu.SemaphoreType.DMA((SLOTS,)),
        ],
        compiler_params=pltpu.CompilerParams(vmem_limit_bytes=VMEM_LIMIT),
        cost_estimate=cost(count, rows, width, trip),
        name="left_terms",
    )(jnp.reshape(place, (1,)), matrices, vecs, weights)


def exchange(values, axis, size, bit):
    return lax.ppermute(values, axis, [(i, i ^ bit) for i in range(size)])


def squares(values):
    return jnp.sum(values * values, axis=0)


def body(n_row, n_col, coefficients, lambdas, right_vecs, left_vecs):
    order = ring_order(n_col)
    weights = chebyshev(lambdas, coefficients.shape[0])
    share = right_vecs.shape[0]
    pair = 2 * share
    left_rows = lax.all_gather(left_vecs, "col", axis=0, tiled=True, axis_index_groups=[order])

    row = lax.axis_index("row").astype(jnp.int32)
    core = lax.rem(row, 2)
    if n_row == 4 and pair % LANES == 0:
        here = row // 2
        there = 1 - here

        def in_order(mine, other):
            return jnp.where(core == 0, jnp.concatenate([mine, other]), jnp.concatenate([other, mine]))

        far = exchange(right_vecs, "row", n_row, 2)
        near_vecs = in_order(right_vecs, exchange(right_vecs, "row", n_row, 1))
        right = right_terms(order, coefficients, near_vecs, weights, here)
        far_vecs = in_order(far, exchange(far, "row", n_row, 1))
        right = right_terms(order, coefficients, far_vecs, weights, there, right)
    else:
        right_cols = lax.all_gather(right_vecs, "row", axis=0, tiled=True)
        right = right_terms(order, coefficients, right_cols, weights, jnp.int32(0))
    right_resid = lax.psum_scatter(right, "col", scatter_dimension=0, tiled=True, axis_index_groups=[order])

    if n_row == 4 and pair % LANES == 0:
        sent = left_terms(order, coefficients, left_rows, weights, there, pair)
        came = exchange(sent, "row", n_row, 2)
        kept = left_terms(order, coefficients, left_rows, weights, here, pair)

        def part(values, which):
            return lax.dynamic_slice_in_dim(values, which * share, share, 0)

        other = part(kept, 1 - core) + part(came, 1 - core)
        left_resid = part(kept, core) + part(came, core) + exchange(other, "row", n_row, 1)
    else:
        left = left_terms(order, coefficients, left_rows, weights, jnp.int32(0), n_row * share)
        left_resid = lax.psum_scatter(left, "row", scatter_dimension=0, tiled=True)

    sums = jnp.stack([squares(right_resid), squares(left_resid)])
    devices = n_row * n_col
    copies = jnp.broadcast_to(sums[None], (devices,) + sums.shape)
    parts = lax.all_to_all(copies, ("row", "col"), split_axis=0, concat_axis=0, tiled=True)
    rows = coefficients.shape[1] * n_row
    root_mean = jnp.sqrt(jnp.sum(parts, axis=0) / rows + epsilon)
    return (right_resid, left_resid, root_mean)


def solution(mesh):
    return jax.shard_map(
        functools.partial(body, mesh.shape["row"], mesh.shape["col"]),
        mesh=mesh,
        in_specs=(P(None, "row", "col"), P(), P(("col", "row"), None), P(("row", "col"), None)),
        out_specs=(P(("row", "col"), None), P(("col", "row"), None), P()),
        check_vma=False,
    )
```

```python
import functools
import jax
import jax.numpy as jnp
from jax import lax
from jax.experimental import pallas as pl
from jax.experimental.pallas import tpu as pltpu
from jax.sharding import PartitionSpec as P

LANES = 128
SLOTS = 3
VMEM_LIMIT = 48 * 2**20

epsilon = 1e-06


def chebyshev(lambdas, count):
    terms = [jnp.ones_like(lambdas), lambdas]
    while len(terms) < count:
        terms.append(2.0 * lambdas * terms[-1] - terms[-2])
    return jnp.stack(terms[:count])


def ring_order(count):
    return list(range(0, count, 2)) + list(range(1, count, 2))[::-1]


def halves(values):
    high = values.astype(jnp.bfloat16)
    return high, (values - high.astype(jnp.float32)).astype(jnp.bfloat16)


def product(left, right, dims):
    def dot(a, b):
        return lax.dot_general(a, b, (dims, ((), ())), preferred_element_type=jnp.float32)

    (left_high, left_low), (right_high, right_low) = left, right
    return dot(left_high, right_high) + dot(left_high, right_low) + dot(left_low, right_high)


def block_copies(matrices_ref, place, buffer, sem):
    width = buffer.shape[2]
    columns = pl.ds(pl.multiple_of(place * width, width), width)

    def copy(term):
        slot = lax.rem(term, SLOTS)
        return pltpu.make_async_copy(matrices_ref.at[term, :, columns], buffer.at[slot], sem.at[slot])

    return copy


def each_matrix(count, copy, step):
    def visit(term, carry):
        copy(term).wait()
        ahead = term + SLOTS - 1

        @pl.when((term > 0) & (ahead < count))
        def _():
            copy(ahead).start()

        step(term)
        return carry

    lax.fori_loop(0, count, visit, 0)


def right_kernel(order, has_total, place_ref, matrices_ref, vecs_ref, weights_ref, *rest):
    out_ref, high, low, buffer, sem = rest[-5:]
    count, rows, _ = matrices_ref.shape
    chunk = rows // len(order)
    copy = block_copies(matrices_ref, place_ref[0], buffer, sem)
    for term in range(min(SLOTS, count)):
        copy(jnp.int32(term)).start()
    out_ref[...] = rest[0][...] if has_total else jnp.zeros_like(out_ref)

    def weigh(term, carry):
        high[term], low[term] = halves(vecs_ref[...] * weights_ref[pl.ds(term, 1), :])
        return carry

    lax.fori_loop(0, count, weigh, 0)

    def step(term):
        terms = product(halves(buffer[lax.rem(term, SLOTS)]), (high[term], low[term]), ((1,), (0,)))
        for at, member in enumerate(order):
            out_ref[at * chunk : (at + 1) * chunk, :] += terms[member * chunk : (member + 1) * chunk, :]

    each_matrix(count, copy, step)


def left_kernel(order, place_ref, matrices_ref, vecs_ref, weights_ref, out_ref, buffer, sem):
    count, rows, _ = matrices_ref.shape
    chunk = rows // len(order)
    copy = block_copies(matrices_ref, place_ref[0], buffer, sem)
    for term in range(min(SLOTS, count)):
        copy(jnp.int32(term)).start()
    out_ref[...] = jnp.zeros_like(out_ref)
    at = [order.index(member) for member in range(len(order))]

    def step(term):
        vecs = jnp.concatenate([vecs_ref[i * chunk : (i + 1) * chunk, :] for i in at], axis=0)
        weighted = halves(vecs * weights_ref[pl.ds(term, 1), :])
        out_ref[...] += product(halves(buffer[lax.rem(term, SLOTS)]), weighted, ((0,), (0,)))

    each_matrix(count, copy, step)


VMEM = pl.BlockSpec(memory_space=pltpu.VMEM)
SMEM = pl.BlockSpec(memory_space=pltpu.SMEM)
ANY = pl.BlockSpec(memory_space=pl.ANY)


def cost(count, rows, width, trip):
    return pl.CostEstimate(
        flops=6 * count * rows * width * trip, bytes_accessed=4 * count * rows * width, transcendentals=0
    )


def right_terms(order, matrices, vecs, weights, place, total=None):
    count, rows, _ = matrices.shape
    width, trip = vecs.shape
    return pl.pallas_call(
        functools.partial(right_kernel, order, total is not None),
        out_shape=jax.ShapeDtypeStruct((rows, trip), jnp.float32),
        in_specs=[SMEM, ANY, VMEM, VMEM] + ([VMEM] if total is not None else []),
        out_specs=VMEM,
        scratch_shapes=[
            pltpu.VMEM((count, width, trip), jnp.bfloat16),
            pltpu.VMEM((count, width, trip), jnp.bfloat16),
            pltpu.VMEM((SLOTS, rows, width), jnp.float32),
            pltpu.SemaphoreType.DMA((SLOTS,)),
        ],
        compiler_params=pltpu.CompilerParams(vmem_limit_bytes=VMEM_LIMIT),
        cost_estimate=cost(count, rows, width, trip),
        name="right_terms",
    )(jnp.reshape(place, (1,)), matrices, vecs, weights, *([total] if total is not None else []))


def left_terms(order, matrices, vecs, weights, place, width):
    count, rows, _ = matrices.shape
    trip = vecs.shape[1]
    return pl.pallas_call(
        functools.partial(left_kernel, order),
        out_shape=jax.ShapeDtypeStruct((width, trip), jnp.float32),
        in_specs=[SMEM, ANY, VMEM, VMEM],
        out_specs=VMEM,
        scratch_shapes=[
            pltpu.VMEM((SLOTS, rows, width), jnp.float32),
            pltpu.SemaphoreType.DMA((SLOTS,)),
        ],
        compiler_params=pltpu.CompilerParams(vmem_limit_bytes=VMEM_LIMIT),
        cost_estimate=cost(count, rows, width, trip),
        name="left_terms",
    )(jnp.reshape(place, (1,)), matrices, vecs, weights)


def exchange(values, axis, size, bit):
    return lax.ppermute(values, axis, [(i, i ^ bit) for i in range(size)])


def squares(values):
    return jnp.sum(values * values, axis=0)


def body(n_row, n_col, coefficients, lambdas, right_vecs, left_vecs):
    order = ring_order(n_col)
    weights = chebyshev(lambdas, coefficients.shape[0])
    share = right_vecs.shape[0]
    pair = 2 * share
    left_rows = lax.all_gather(left_vecs, "col", axis=0, tiled=True, axis_index_groups=[order])

    row = lax.axis_index("row").astype(jnp.int32)
    core = lax.rem(row, 2)
    if n_row == 4 and pair % LANES == 0:
        here = row // 2
        there = 1 - here
        other = exchange(right_vecs, "row", n_row, 1)
        near_vecs = jnp.where(core == 0, jnp.concatenate([right_vecs, other]), jnp.concatenate([other, right_vecs]))
        far_vecs = exchange(near_vecs, "row", n_row, 2)
        right = right_terms(order, coefficients, near_vecs, weights, here)
        right = right_terms(order, coefficients, far_vecs, weights, there, right)
    else:
        right_cols = lax.all_gather(right_vecs, "row", axis=0, tiled=True)
        right = right_terms(order, coefficients, right_cols, weights, jnp.int32(0))
    right_resid = lax.psum_scatter(right, "col", scatter_dimension=0, tiled=True, axis_index_groups=[order])

    if n_row == 4 and pair % LANES == 0:
        sent = left_terms(order, coefficients, left_rows, weights, there, pair)
        came = exchange(sent, "row", n_row, 2)
        kept = left_terms(order, coefficients, left_rows, weights, here, pair)

        def part(values, which):
            return lax.dynamic_slice_in_dim(values, which * share, share, 0)

        other = part(kept, 1 - core) + part(came, 1 - core)
        left_resid = part(kept, core) + part(came, core) + exchange(other, "row", n_row, 1)
    else:
        left = left_terms(order, coefficients, left_rows, weights, jnp.int32(0), n_row * share)
        left_resid = lax.psum_scatter(left, "row", scatter_dimension=0, tiled=True)

    sums = jnp.stack([squares(right_resid), squares(left_resid)])
    devices = n_row * n_col
    copies = jnp.broadcast_to(sums[None], (devices,) + sums.shape)
    parts = lax.all_to_all(copies, ("row", "col"), split_axis=0, concat_axis=0, tiled=True)
    rows = coefficients.shape[1] * n_row
    root_mean = jnp.sqrt(jnp.sum(parts, axis=0) / rows + epsilon)
    return (right_resid, left_resid, root_mean)


def solution(mesh):
    return jax.shard_map(
        functools.partial(body, mesh.shape["row"], mesh.shape["col"]),
        mesh=mesh,
        in_specs=(P(None, "row", "col"), P(), P(("col", "row"), None), P(("row", "col"), None)),
        out_specs=(P(("row", "col"), None), P(("col", "row"), None), P()),
        check_vma=False,
    )
```

```python
import functools
import jax
import jax.numpy as jnp
from jax import lax
from jax.experimental import pallas as pl
from jax.experimental.pallas import tpu as pltpu
from jax.sharding import PartitionSpec as P

LANES = 128
SLOTS = 3
VMEM_LIMIT = 48 * 2**20

epsilon = 1e-06


def fill_weights(lambdas_ref, weights):
    lambdas = lambdas_ref[...]
    terms = [jnp.ones_like(lambdas), lambdas]
    while len(terms) < weights.shape[0]:
        terms.append(2.0 * lambdas * terms[-1] - terms[-2])
    for term in range(weights.shape[0]):
        weights[term : term + 1, :] = terms[term]


def ring_order(count):
    return list(range(0, count, 2)) + list(range(1, count, 2))[::-1]


def halves(values):
    high = values.astype(jnp.bfloat16)
    return high, (values - high.astype(jnp.float32)).astype(jnp.bfloat16)


def product(left, right, dims):
    def dot(a, b):
        return lax.dot_general(a, b, (dims, ((), ())), preferred_element_type=jnp.float32)

    (left_high, left_low), (right_high, right_low) = left, right
    return dot(left_high, right_high) + dot(left_high, right_low) + dot(left_low, right_high)


def visit_matrices(matrices_ref, place, buffer, sem, piece_sem, prepare, work_piece, work):
    count, rows, _ = matrices_ref.shape
    width = buffer.shape[2]
    columns = pl.ds(pl.multiple_of(place * width, width), width)
    pieces = piece_sem.shape[0]
    depth = rows // pieces

    def copy(term):
        slot = lax.rem(term, SLOTS)
        return pltpu.make_async_copy(matrices_ref.at[term, :, columns], buffer.at[slot], sem.at[slot])

    def copy_piece(piece):
        part = pl.ds(pl.multiple_of(piece * depth, depth), depth)
        return pltpu.make_async_copy(matrices_ref.at[0, part, columns], buffer.at[0, part], piece_sem.at[piece])

    for piece in range(pieces):
        copy_piece(jnp.int32(piece)).start()
    for term in range(1, min(SLOTS, count)):
        copy(jnp.int32(term)).start()
    prepare()

    def visit_piece(piece, carry):
        copy_piece(piece).wait()
        work_piece(piece, buffer[0, pl.ds(pl.multiple_of(piece * depth, depth), depth), :])
        return carry

    lax.fori_loop(0, pieces, visit_piece, 0)

    def visit(term, carry):
        copy(term).wait()
        ahead = term + SLOTS - 1

        @pl.when(ahead < count)
        def _():
            copy(ahead).start()

        work(term, buffer[lax.rem(term, SLOTS)])
        return carry

    lax.fori_loop(1, count, visit, 0)


def right_kernel(order, n_vecs, places_ref, matrices_ref, lambdas_ref, *rest):
    vecs_refs, total_refs = rest[:n_vecs], rest[n_vecs:-7]
    out_ref, high, low, weights, buffer, sem, piece_sem = rest[-7:]
    count, rows, _ = matrices_ref.shape
    chunk = rows // len(order)

    def prepare():
        fill_weights(lambdas_ref, weights)
        for at, vecs_ref in enumerate(vecs_refs):
            share = vecs_ref.shape[0]
            place = pl.ds(pl.multiple_of(places_ref[1 + at] * share, share), share)

            def weigh(term, carry):
                high[term, place], low[term, place] = halves(vecs_ref[...] * weights[pl.ds(term, 1), :])
                return carry

            lax.fori_loop(0, count, weigh, 0)
        out_ref[...] = total_refs[0][...] if total_refs else jnp.zeros_like(out_ref)

    def work_piece(piece, block):
        terms = product(halves(block), (high[0], low[0]), ((1,), (0,)))
        for part, at in enumerate((piece, len(order) - 1 - piece)):
            out_ref[pl.ds(pl.multiple_of(at * chunk, chunk), chunk), :] += terms[part * chunk : (part + 1) * chunk, :]

    def work(term, block):
        terms = product(halves(block), (high[term], low[term]), ((1,), (0,)))
        for at, member in enumerate(order):
            out_ref[at * chunk : (at + 1) * chunk, :] += terms[member * chunk : (member + 1) * chunk, :]

    visit_matrices(matrices_ref, places_ref[0], buffer, sem, piece_sem, prepare, work_piece, work)


def left_kernel(order, places_ref, matrices_ref, lambdas_ref, vecs_hbm, out_ref, vecs, weights, buffer, sem, piece_sem, vecs_sem):
    count, rows, _ = matrices_ref.shape
    chunk = rows // len(order)
    fetch = pltpu.make_async_copy(vecs_hbm, vecs, vecs_sem)
    fetch.start()

    def prepare():
        fill_weights(lambdas_ref, weights)
        out_ref[...] = jnp.zeros_like(out_ref)
        fetch.wait()

    def work_piece(piece, block):
        places = [pl.ds(pl.multiple_of(at * chunk, chunk), chunk) for at in (piece, len(order) - 1 - piece)]
        held = jnp.concatenate([vecs[place, :] for place in places], axis=0)
        out_ref[...] += product(halves(block), halves(held * weights[0:1, :]), ((0,), (0,)))

    def work(term, block):
        places = [order.index(member) for member in range(len(order))]
        held = jnp.concatenate([vecs[at * chunk : (at + 1) * chunk, :] for at in places], axis=0)
        weighted = halves(held * weights[pl.ds(term, 1), :])
        out_ref[...] += product(halves(block), weighted, ((0,), (0,)))

    visit_matrices(matrices_ref, places_ref[0], buffer, sem, piece_sem, prepare, work_piece, work)


VMEM = pl.BlockSpec(memory_space=pltpu.VMEM)
SMEM = pl.BlockSpec(memory_space=pltpu.SMEM)
ANY = pl.BlockSpec(memory_space=pl.ANY)
HBM = pl.BlockSpec(memory_space=pltpu.HBM)


def cost(count, rows, width, trip):
    return pl.CostEstimate(
        flops=6 * count * rows * width * trip, bytes_accessed=4 * count * rows * width, transcendentals=0
    )


def right_terms(order, matrices, lambdas, vecs, places, total=()):
    count, rows, _ = matrices.shape
    trip = lambdas.shape[1]
    width = sum(part.shape[0] for part in vecs)
    pieces = len(order) // 2
    return pl.pallas_call(
        functools.partial(right_kernel, order, len(vecs)),
        out_shape=jax.ShapeDtypeStruct((rows, trip), jnp.float32),
        in_specs=[SMEM, ANY, VMEM] + [VMEM] * (len(vecs) + len(total)),
        out_specs=VMEM,
        scratch_shapes=[
            pltpu.VMEM((count, width, trip), jnp.bfloat16),
            pltpu.VMEM((count, width, trip), jnp.bfloat16),
            pltpu.VMEM((count, trip), jnp.float32),
            pltpu.VMEM((SLOTS, rows, width), jnp.float32),
            pltpu.SemaphoreType.DMA((SLOTS,)),
            pltpu.SemaphoreType.DMA((pieces,)),
        ],
        compiler_params=pltpu.CompilerParams(vmem_limit_bytes=VMEM_LIMIT),
        cost_estimate=cost(count, rows, width, trip),
        name="right_terms",
    )(jnp.stack(places), matrices, lambdas, *vecs, *total)


def left_terms(order, matrices, lambdas, vecs, place, width):
    count, rows, _ = matrices.shape
    trip = vecs.shape[1]
    pieces = len(order) // 2
    return pl.pallas_call(
        functools.partial(left_kernel, order),
        out_shape=jax.ShapeDtypeStruct((width, trip), jnp.float32),
        in_specs=[SMEM, ANY, VMEM, HBM],
        out_specs=VMEM,
        scratch_shapes=[
            pltpu.VMEM((rows, trip), jnp.float32),
            pltpu.VMEM((count, trip), jnp.float32),
            pltpu.VMEM((SLOTS, rows, width), jnp.float32),
            pltpu.SemaphoreType.DMA((SLOTS,)),
            pltpu.SemaphoreType.DMA((pieces,)),
            pltpu.SemaphoreType.DMA,
        ],
        compiler_params=pltpu.CompilerParams(vmem_limit_bytes=VMEM_LIMIT),
        cost_estimate=cost(count, rows, width, trip),
        name="left_terms",
    )(jnp.stack([place]), matrices, lambdas, vecs)


def exchange(values, axis, size, bit):
    return lax.ppermute(values, axis, [(i, i ^ bit) for i in range(size)])


def squares(values):
    return jnp.sum(values * values, axis=0)


def body(n_row, n_col, coefficients, lambdas, right_vecs, left_vecs):
    order = ring_order(n_col)
    lambdas = lambdas[None]
    share = right_vecs.shape[0]
    pair = 2 * share
    left_rows = lax.all_gather(left_vecs, "col", axis=0, tiled=True, axis_index_groups=[order])

    row = lax.axis_index("row").astype(jnp.int32)
    core = lax.rem(row, 2)
    in_pairs = n_row == 4 and pair % LANES == 0
    if in_pairs:
        here, there = row // 2, 1 - row // 2
        other = exchange(right_vecs, "row", n_row, 1)
        far = [exchange(right_vecs, "row", n_row, bit) for bit in (2, 3)]
        places = [core, 1 - core]
        right = right_terms(order, coefficients, lambdas, [right_vecs, other], [here] + places)
        right = right_terms(order, coefficients, lambdas, far, [there] + places, [right])
    else:
        right_cols = lax.all_gather(right_vecs, "row", axis=0, tiled=True)
        right = right_terms(order, coefficients, lambdas, [right_cols], [jnp.int32(0)] * 2)
    right_resid = lax.psum_scatter(right, "col", scatter_dimension=0, tiled=True, axis_index_groups=[order])
    right_squares = squares(right_resid)

    if in_pairs:
        sent = left_terms(order, coefficients, lambdas, left_rows, there, pair)
        came = exchange(sent, "row", n_row, 2)
        kept = left_terms(order, coefficients, lambdas, left_rows, here, pair)

        def part(values, which):
            return lax.dynamic_slice_in_dim(values, which * share, share, 0)

        last = exchange(part(kept, 1 - core) + part(came, 1 - core), "row", n_row, 1)
        last, right_squares = lax.optimization_barrier((last, right_squares))
        left_resid = part(kept, core) + part(came, core) + last
    else:
        left = left_terms(order, coefficients, lambdas, left_rows, jnp.int32(0), n_row * share)
        left_resid = lax.psum_scatter(left, "row", scatter_dimension=0, tiled=True)

    sums = jnp.stack([right_squares, squares(left_resid)])
    devices = n_row * n_col
    copies = jnp.broadcast_to(sums[None], (devices,) + sums.shape)
    parts = lax.all_to_all(copies, ("row", "col"), split_axis=0, concat_axis=0, tiled=True)
    rows = coefficients.shape[1] * n_row
    root_mean = jnp.sqrt(jnp.sum(parts, axis=0) / rows + epsilon)
    return (right_resid, left_resid, root_mean)


def solution(mesh):
    return jax.shard_map(
        functools.partial(body, mesh.shape["row"], mesh.shape["col"]),
        mesh=mesh,
        in_specs=(P(None, "row", "col"), P(), P(("col", "row"), None), P(("row", "col"), None)),
        out_specs=(P(("row", "col"), None), P(("col", "row"), None), P()),
        check_vma=False,
    )
```

```python
import functools
import jax
import jax.numpy as jnp
from jax import lax
from jax.experimental import pallas as pl
from jax.experimental.pallas import tpu as pltpu
from jax.sharding import PartitionSpec as P

LANES = 128
SLOTS = 3
VMEM_LIMIT = 48 * 2**20

epsilon = 1e-06


def chebyshev(lambdas, count):
    terms = [jnp.ones_like(lambdas), lambdas]
    while len(terms) < count:
        terms.append(2.0 * lambdas * terms[-1] - terms[-2])
    return jnp.stack(terms[:count])


def ring_order(count):
    return list(range(0, count, 2)) + list(range(1, count, 2))[::-1]


def halves(values):
    high = values.astype(jnp.bfloat16)
    return high, (values - high.astype(jnp.float32)).astype(jnp.bfloat16)


def product(left, right, dims):
    def dot(a, b):
        return lax.dot_general(a, b, (dims, ((), ())), preferred_element_type=jnp.float32)

    (left_high, left_low), (right_high, right_low) = left, right
    return dot(left_high, right_high) + dot(left_high, right_low) + dot(left_low, right_high)


def block_copies(matrices_ref, place, buffer, sem):
    width = buffer.shape[2]
    columns = pl.ds(pl.multiple_of(place * width, width), width)

    def copy(term):
        slot = lax.rem(term, SLOTS)
        return pltpu.make_async_copy(matrices_ref.at[term, :, columns], buffer.at[slot], sem.at[slot])

    return copy


def each_matrix(first, count, copy, step):
    def visit(term, carry):
        copy(term).wait()
        ahead = term + SLOTS - 1

        @pl.when((term > 0) & (ahead < count))
        def _():
            copy(ahead).start()

        step(term)
        return carry

    lax.fori_loop(first, count, visit, 0)


def right_kernel(order, has_total, place_ref, matrices_ref, vecs_ref, weights_ref, *rest):
    out_ref, high, low, buffer, sem, piece_sem = rest[-6:]
    count, rows, _ = matrices_ref.shape
    chunk = rows // len(order)
    copy = block_copies(matrices_ref, place_ref[0], buffer, sem)
    depth = 2 * chunk
    width = buffer.shape[2]
    columns = pl.ds(pl.multiple_of(place_ref[0] * width, width), width)

    def copy_piece(piece):
        part = pl.ds(pl.multiple_of(piece * depth, depth), depth)
        return pltpu.make_async_copy(matrices_ref.at[0, part, columns], buffer.at[0, part], piece_sem.at[piece])

    for piece in range(rows // depth):
        copy_piece(jnp.int32(piece)).start()
    for term in range(1, min(SLOTS, count)):
        copy(jnp.int32(term)).start()
    out_ref[...] = rest[0][...] if has_total else jnp.zeros_like(out_ref)

    def weigh(term, carry):
        high[term], low[term] = halves(vecs_ref[...] * weights_ref[pl.ds(term, 1), :])
        return carry

    lax.fori_loop(0, count, weigh, 0)

    def step_piece(piece, carry):
        copy_piece(piece).wait()
        block = buffer[0, pl.ds(pl.multiple_of(piece * depth, depth), depth), :]
        terms = product(halves(block), (high[0], low[0]), ((1,), (0,)))
        for part, at in enumerate((piece, len(order) - 1 - piece)):
            out_ref[pl.ds(pl.multiple_of(at * chunk, chunk), chunk), :] += terms[part * chunk : (part + 1) * chunk, :]
        return carry

    lax.fori_loop(0, rows // depth, step_piece, 0)

    def step(term):
        terms = product(halves(buffer[lax.rem(term, SLOTS)]), (high[term], low[term]), ((1,), (0,)))
        for at, member in enumerate(order):
            out_ref[at * chunk : (at + 1) * chunk, :] += terms[member * chunk : (member + 1) * chunk, :]

    each_matrix(1, count, copy, step)


def left_kernel(order, place_ref, matrices_ref, vecs_ref, weights_ref, out_ref, buffer, sem):
    count, rows, _ = matrices_ref.shape
    chunk = rows // len(order)
    copy = block_copies(matrices_ref, place_ref[0], buffer, sem)
    for term in range(min(SLOTS, count)):
        copy(jnp.int32(term)).start()
    out_ref[...] = jnp.zeros_like(out_ref)
    at = [order.index(member) for member in range(len(order))]

    def step(term):
        vecs = jnp.concatenate([vecs_ref[i * chunk : (i + 1) * chunk, :] for i in at], axis=0)
        weighted = halves(vecs * weights_ref[pl.ds(term, 1), :])
        out_ref[...] += product(halves(buffer[lax.rem(term, SLOTS)]), weighted, ((0,), (0,)))

    each_matrix(0, count, copy, step)


VMEM = pl.BlockSpec(memory_space=pltpu.VMEM)
SMEM = pl.BlockSpec(memory_space=pltpu.SMEM)
ANY = pl.BlockSpec(memory_space=pl.ANY)


def cost(count, rows, width, trip):
    return pl.CostEstimate(
        flops=6 * count * rows * width * trip, bytes_accessed=4 * count * rows * width, transcendentals=0
    )


def right_terms(order, matrices, vecs, weights, place, total=None):
    count, rows, _ = matrices.shape
    width, trip = vecs.shape
    return pl.pallas_call(
        functools.partial(right_kernel, order, total is not None),
        out_shape=jax.ShapeDtypeStruct((rows, trip), jnp.float32),
        in_specs=[SMEM, ANY, VMEM, VMEM] + ([VMEM] if total is not None else []),
        out_specs=VMEM,
        scratch_shapes=[
            pltpu.VMEM((count, width, trip), jnp.bfloat16),
            pltpu.VMEM((count, width, trip), jnp.bfloat16),
            pltpu.VMEM((SLOTS, rows, width), jnp.float32),
            pltpu.SemaphoreType.DMA((SLOTS,)),
            pltpu.SemaphoreType.DMA((len(order) // 2,)),
        ],
        compiler_params=pltpu.CompilerParams(vmem_limit_bytes=VMEM_LIMIT),
        cost_estimate=cost(count, rows, width, trip),
        name="right_terms",
    )(jnp.reshape(place, (1,)), matrices, vecs, weights, *([total] if total is not None else []))


def left_terms(order, matrices, vecs, weights, place, width):
    count, rows, _ = matrices.shape
    trip = vecs.shape[1]
    return pl.pallas_call(
        functools.partial(left_kernel, order),
        out_shape=jax.ShapeDtypeStruct((width, trip), jnp.float32),
        in_specs=[SMEM, ANY, VMEM, VMEM],
        out_specs=VMEM,
        scratch_shapes=[
            pltpu.VMEM((SLOTS, rows, width), jnp.float32),
            pltpu.SemaphoreType.DMA((SLOTS,)),
        ],
        compiler_params=pltpu.CompilerParams(vmem_limit_bytes=VMEM_LIMIT),
        cost_estimate=cost(count, rows, width, trip),
        name="left_terms",
    )(jnp.reshape(place, (1,)), matrices, vecs, weights)


def exchange(values, axis, size, bit):
    return lax.ppermute(values, axis, [(i, i ^ bit) for i in range(size)])


def squares(values):
    return jnp.sum(values * values, axis=0)


def body(n_row, n_col, coefficients, lambdas, right_vecs, left_vecs):
    order = ring_order(n_col)
    weights = chebyshev(lambdas, coefficients.shape[0])
    share = right_vecs.shape[0]
    pair = 2 * share
    left_rows = lax.all_gather(left_vecs, "col", axis=0, tiled=True, axis_index_groups=[order])

    row = lax.axis_index("row").astype(jnp.int32)
    core = lax.rem(row, 2)
    if n_row == 4 and pair % LANES == 0:
        here = row // 2
        there = 1 - here
        other = exchange(right_vecs, "row", n_row, 1)
        near_vecs = jnp.where(core == 0, jnp.concatenate([right_vecs, other]), jnp.concatenate([other, right_vecs]))
        far_vecs = exchange(near_vecs, "row", n_row, 2)
        right = right_terms(order, coefficients, near_vecs, weights, here)
        right = right_terms(order, coefficients, far_vecs, weights, there, right)
    else:
        right_cols = lax.all_gather(right_vecs, "row", axis=0, tiled=True)
        right = right_terms(order, coefficients, right_cols, weights, jnp.int32(0))
    right_resid = lax.psum_scatter(right, "col", scatter_dimension=0, tiled=True, axis_index_groups=[order])
    right_squares = squares(right_resid)

    if n_row == 4 and pair % LANES == 0:
        sent = left_terms(order, coefficients, left_rows, weights, there, pair)
        came = exchange(sent, "row", n_row, 2)
        kept = left_terms(order, coefficients, left_rows, weights, here, pair)

        def part(values, which):
            return lax.dynamic_slice_in_dim(values, which * share, share, 0)

        other = part(kept, 1 - core) + part(came, 1 - core)
        last, right_squares = lax.optimization_barrier((exchange(other, "row", n_row, 1), right_squares))
        left_resid = part(kept, core) + part(came, core) + last
    else:
        left = left_terms(order, coefficients, left_rows, weights, jnp.int32(0), n_row * share)
        left_resid = lax.psum_scatter(left, "row", scatter_dimension=0, tiled=True)

    sums = jnp.stack([right_squares, squares(left_resid)])
    devices = n_row * n_col
    copies = jnp.broadcast_to(sums[None], (devices,) + sums.shape)
    parts = lax.all_to_all(copies, ("row", "col"), split_axis=0, concat_axis=0, tiled=True)
    rows = coefficients.shape[1] * n_row
    root_mean = jnp.sqrt(jnp.sum(parts, axis=0) / rows + epsilon)
    return (right_resid, left_resid, root_mean)


def solution(mesh):
    return jax.shard_map(
        functools.partial(body, mesh.shape["row"], mesh.shape["col"]),
        mesh=mesh,
        in_specs=(P(None, "row", "col"), P(), P(("col", "row"), None), P(("row", "col"), None)),
        out_specs=(P(("row", "col"), None), P(("col", "row"), None), P()),
        check_vma=False,
    )
```

```python
import functools
import jax
import jax.numpy as jnp
from jax import lax
from jax.experimental import pallas as pl
from jax.experimental.pallas import tpu as pltpu
from jax.sharding import PartitionSpec as P

LANES = 128
SLOTS = 3
VMEM_LIMIT = 48 * 2**20

epsilon = 1e-06


def chebyshev(lambdas, count):
    terms = [jnp.ones_like(lambdas), lambdas]
    while len(terms) < count:
        terms.append(2.0 * lambdas * terms[-1] - terms[-2])
    return jnp.stack(terms[:count])


def ring_order(count):
    return list(range(0, count, 2)) + list(range(1, count, 2))[::-1]


def halves(values):
    high = values.astype(jnp.bfloat16)
    return high, (values - high.astype(jnp.float32)).astype(jnp.bfloat16)


def product(left, right, dims):
    def dot(a, b):
        return lax.dot_general(a, b, (dims, ((), ())), preferred_element_type=jnp.float32)

    (left_high, left_low), (right_high, right_low) = left, right
    return dot(left_high, right_high) + dot(left_high, right_low) + dot(left_low, right_high)


def block_copies(matrices_ref, place, buffer, sem):
    width = buffer.shape[2]
    columns = pl.ds(pl.multiple_of(place * width, width), width)

    def copy(term):
        slot = lax.rem(term, SLOTS)
        return pltpu.make_async_copy(matrices_ref.at[term, :, columns], buffer.at[slot], sem.at[slot])

    return copy


def each_matrix(first, count, copy, step):
    def visit(term, carry):
        copy(term).wait()
        ahead = term + SLOTS - 1

        @pl.when((term > 0) & (ahead < count))
        def _():
            copy(ahead).start()

        step(term)
        return carry

    lax.fori_loop(first, count, visit, 0)


def right_kernel(order, has_total, place_ref, matrices_ref, vecs_ref, weights_ref, *rest):
    out_ref, high, low, buffer, sem, piece_sem = rest[-6:]
    count, rows, _ = matrices_ref.shape
    chunk = rows // len(order)
    copy = block_copies(matrices_ref, place_ref[0], buffer, sem)
    depth = 2 * chunk
    width = buffer.shape[2]
    columns = pl.ds(pl.multiple_of(place_ref[0] * width, width), width)

    def copy_piece(piece):
        part = pl.ds(pl.multiple_of(piece * depth, depth), depth)
        return pltpu.make_async_copy(matrices_ref.at[0, part, columns], buffer.at[0, part], piece_sem.at[piece])

    for piece in range(rows // depth):
        copy_piece(jnp.int32(piece)).start()
    for term in range(1, min(SLOTS, count)):
        copy(jnp.int32(term)).start()
    out_ref[...] = rest[0][...] if has_total else jnp.zeros_like(out_ref)

    def weigh(term, carry):
        high[term], low[term] = halves(vecs_ref[...] * weights_ref[pl.ds(term, 1), :])
        return carry

    lax.fori_loop(0, count, weigh, 0)

    def step_piece(piece, carry):
        copy_piece(piece).wait()
        block = buffer[0, pl.ds(pl.multiple_of(piece * depth, depth), depth), :]
        terms = product(halves(block), (high[0], low[0]), ((1,), (0,)))
        for part, at in enumerate((piece, len(order) - 1 - piece)):
            out_ref[pl.ds(pl.multiple_of(at * chunk, chunk), chunk), :] += terms[part * chunk : (part + 1) * chunk, :]
        return carry

    lax.fori_loop(0, rows // depth, step_piece, 0)

    def step(term):
        terms = product(halves(buffer[lax.rem(term, SLOTS)]), (high[term], low[term]), ((1,), (0,)))
        for at, member in enumerate(order):
            out_ref[at * chunk : (at + 1) * chunk, :] += terms[member * chunk : (member + 1) * chunk, :]

    each_matrix(1, count, copy, step)


def left_kernel(order, place_ref, matrices_ref, high_ref, low_ref, weights_ref, out_ref, buffer, sem):
    count, rows, _ = matrices_ref.shape
    chunk = rows // len(order)
    copy = block_copies(matrices_ref, place_ref[0], buffer, sem)
    for term in range(min(SLOTS, count)):
        copy(jnp.int32(term)).start()
    out_ref[...] = jnp.zeros_like(out_ref)
    at = [order.index(member) for member in range(len(order))]

    def step(term):
        vecs = [
            jnp.concatenate([ref[i * chunk : (i + 1) * chunk, :] for i in at], axis=0) for ref in (high_ref, low_ref)
        ]
        terms = product(halves(buffer[lax.rem(term, SLOTS)]), vecs, ((0,), (0,)))
        out_ref[...] += terms * weights_ref[pl.ds(term, 1), :]

    each_matrix(0, count, copy, step)


VMEM = pl.BlockSpec(memory_space=pltpu.VMEM)
SMEM = pl.BlockSpec(memory_space=pltpu.SMEM)
ANY = pl.BlockSpec(memory_space=pl.ANY)


def cost(count, rows, width, trip):
    return pl.CostEstimate(
        flops=6 * count * rows * width * trip, bytes_accessed=4 * count * rows * width, transcendentals=0
    )


def right_terms(order, matrices, vecs, weights, place, total=None):
    count, rows, _ = matrices.shape
    width, trip = vecs.shape
    return pl.pallas_call(
        functools.partial(right_kernel, order, total is not None),
        out_shape=jax.ShapeDtypeStruct((rows, trip), jnp.float32),
        in_specs=[SMEM, ANY, VMEM, VMEM] + ([VMEM] if total is not None else []),
        out_specs=VMEM,
        scratch_shapes=[
            pltpu.VMEM((count, width, trip), jnp.bfloat16),
            pltpu.VMEM((count, width, trip), jnp.bfloat16),
            pltpu.VMEM((SLOTS, rows, width), jnp.float32),
            pltpu.SemaphoreType.DMA((SLOTS,)),
            pltpu.SemaphoreType.DMA((len(order) // 2,)),
        ],
        compiler_params=pltpu.CompilerParams(vmem_limit_bytes=VMEM_LIMIT),
        cost_estimate=cost(count, rows, width, trip),
        name="right_terms",
    )(jnp.reshape(place, (1,)), matrices, vecs, weights, *([total] if total is not None else []))


def left_terms(order, matrices, vecs, weights, place, width):
    count, rows, _ = matrices.shape
    trip = vecs[0].shape[1]
    return pl.pallas_call(
        functools.partial(left_kernel, order),
        out_shape=jax.ShapeDtypeStruct((width, trip), jnp.float32),
        in_specs=[SMEM, ANY, VMEM, VMEM, VMEM],
        out_specs=VMEM,
        scratch_shapes=[
            pltpu.VMEM((SLOTS, rows, width), jnp.float32),
            pltpu.SemaphoreType.DMA((SLOTS,)),
        ],
        compiler_params=pltpu.CompilerParams(vmem_limit_bytes=VMEM_LIMIT),
        cost_estimate=cost(count, rows, width, trip),
        name="left_terms",
    )(jnp.reshape(place, (1,)), matrices, *vecs, weights)


def exchange(values, axis, size, bit):
    return lax.ppermute(values, axis, [(i, i ^ bit) for i in range(size)])


def squares(values):
    return jnp.sum(values * values, axis=0)


def body(n_row, n_col, coefficients, lambdas, right_vecs, left_vecs):
    order = ring_order(n_col)
    weights = chebyshev(lambdas, coefficients.shape[0])
    share = right_vecs.shape[0]
    pair = 2 * share
    left_rows = lax.all_gather(left_vecs, "col", axis=0, tiled=True, axis_index_groups=[order])

    left_high = lax.reduce_precision(left_rows, 8, 7)
    left_halves = (left_high.astype(jnp.bfloat16), (left_rows - left_high).astype(jnp.bfloat16))

    row = lax.axis_index("row").astype(jnp.int32)
    core = lax.rem(row, 2)
    if n_row == 4 and pair % LANES == 0:
        here = row // 2
        there = 1 - here
        other = exchange(right_vecs, "row", n_row, 1)
        near_vecs = jnp.where(core == 0, jnp.concatenate([right_vecs, other]), jnp.concatenate([other, right_vecs]))
        far_vecs = exchange(near_vecs, "row", n_row, 2)
        right = right_terms(order, coefficients, near_vecs, weights, here)
        right = right_terms(order, coefficients, far_vecs, weights, there, right)
    else:
        right_cols = lax.all_gather(right_vecs, "row", axis=0, tiled=True)
        right = right_terms(order, coefficients, right_cols, weights, jnp.int32(0))
    right_resid = lax.psum_scatter(right, "col", scatter_dimension=0, tiled=True, axis_index_groups=[order])
    right_squares = squares(right_resid)

    if n_row == 4 and pair % LANES == 0:
        sent = left_terms(order, coefficients, left_halves, weights, there, pair)
        came = exchange(sent, "row", n_row, 2)
        kept = left_terms(order, coefficients, left_halves, weights, here, pair)

        def part(values, which):
            return lax.dynamic_slice_in_dim(values, which * share, share, 0)

        other = part(kept, 1 - core) + part(came, 1 - core)
        last, right_squares = lax.optimization_barrier((exchange(other, "row", n_row, 1), right_squares))
        left_resid = part(kept, core) + part(came, core) + last
    else:
        left = left_terms(order, coefficients, left_halves, weights, jnp.int32(0), n_row * share)
        left_resid = lax.psum_scatter(left, "row", scatter_dimension=0, tiled=True)

    sums = jnp.stack([right_squares, squares(left_resid)])
    devices = n_row * n_col
    copies = jnp.broadcast_to(sums[None], (devices,) + sums.shape)
    parts = lax.all_to_all(copies, ("row", "col"), split_axis=0, concat_axis=0, tiled=True)
    rows = coefficients.shape[1] * n_row
    root_mean = jnp.sqrt(jnp.sum(parts, axis=0) / rows + epsilon)
    return (right_resid, left_resid, root_mean)


def solution(mesh):
    return jax.shard_map(
        functools.partial(body, mesh.shape["row"], mesh.shape["col"]),
        mesh=mesh,
        in_specs=(P(None, "row", "col"), P(), P(("col", "row"), None), P(("row", "col"), None)),
        out_specs=(P(("row", "col"), None), P(("col", "row"), None), P()),
        check_vma=False,
    )
```

```python
import functools
import jax
import jax.numpy as jnp
from jax import lax
from jax.experimental import pallas as pl
from jax.experimental.pallas import tpu as pltpu
from jax.sharding import PartitionSpec as P

LANES = 128
SLOTS = 3
VMEM_LIMIT = 48 * 2**20

epsilon = 1e-06


def chebyshev(lambdas, count):
    terms = [jnp.ones_like(lambdas), lambdas]
    while len(terms) < count:
        terms.append(2.0 * lambdas * terms[-1] - terms[-2])
    return jnp.stack(terms[:count])


def ring_order(count):
    return list(range(0, count, 2)) + list(range(1, count, 2))[::-1]


def halves(values):
    high = values.astype(jnp.bfloat16)
    return high, (values - high.astype(jnp.float32)).astype(jnp.bfloat16)


def product(left, right, dims):
    def dot(a, b):
        return lax.dot_general(a, b, (dims, ((), ())), preferred_element_type=jnp.float32)

    (left_high, left_low), (right_high, right_low) = left, right
    return dot(left_high, right_high) + dot(left_high, right_low) + dot(left_low, right_high)


def block_copies(matrices_ref, place, buffer, sem):
    width = buffer.shape[2]
    columns = pl.ds(pl.multiple_of(place * width, width), width)

    def copy(term):
        slot = lax.rem(term, SLOTS)
        return pltpu.make_async_copy(matrices_ref.at[term, :, columns], buffer.at[slot], sem.at[slot])

    return copy


def piece_copies(matrices_ref, place, buffer, sem):
    width = buffer.shape[2]
    columns = pl.ds(pl.multiple_of(place * width, width), width)
    depth = matrices_ref.shape[1] // sem.shape[0]

    def copy_piece(piece):
        part = pl.ds(pl.multiple_of(piece * depth, depth), depth)
        return pltpu.make_async_copy(matrices_ref.at[0, part, columns], buffer.at[0, part], sem.at[piece])

    return copy_piece, depth


def each_matrix(first, count, copy, step):
    def visit(term, carry):
        copy(term).wait()
        ahead = term + SLOTS - 1

        @pl.when((term > 0) & (ahead < count))
        def _():
            copy(ahead).start()

        step(term)
        return carry

    lax.fori_loop(first, count, visit, 0)


def right_kernel(order, has_total, place_ref, matrices_ref, vecs_ref, weights_ref, *rest):
    out_ref, high, low, buffer, sem, piece_sem = rest[-6:]
    count, rows, _ = matrices_ref.shape
    chunk = rows // len(order)
    copy = block_copies(matrices_ref, place_ref[0], buffer, sem)
    copy_piece, depth = piece_copies(matrices_ref, place_ref[0], buffer, piece_sem)
    for piece in range(rows // depth):
        copy_piece(jnp.int32(piece)).start()
    for term in range(1, min(SLOTS, count)):
        copy(jnp.int32(term)).start()
    out_ref[...] = rest[0][...] if has_total else jnp.zeros_like(out_ref)

    def weigh(term, carry):
        high[term], low[term] = halves(vecs_ref[...] * weights_ref[pl.ds(term, 1), :])
        return carry

    lax.fori_loop(0, count, weigh, 0)

    def step_piece(piece, carry):
        copy_piece(piece).wait()
        block = buffer[0, pl.ds(pl.multiple_of(piece * depth, depth), depth), :]
        terms = product(halves(block), (high[0], low[0]), ((1,), (0,)))
        for part, at in enumerate((piece, len(order) - 1 - piece)):
            out_ref[pl.ds(pl.multiple_of(at * chunk, chunk), chunk), :] += terms[part * chunk : (part + 1) * chunk, :]
        return carry

    lax.fori_loop(0, rows // depth, step_piece, 0)

    def step(term):
        terms = product(halves(buffer[lax.rem(term, SLOTS)]), (high[term], low[term]), ((1,), (0,)))
        for at, member in enumerate(order):
            out_ref[at * chunk : (at + 1) * chunk, :] += terms[member * chunk : (member + 1) * chunk, :]

    each_matrix(1, count, copy, step)


def left_kernel(order, place_ref, matrices_ref, high_ref, low_ref, weights_ref, out_ref, buffer, sem, piece_sem):
    count, rows, _ = matrices_ref.shape
    chunk = rows // len(order)
    copy = block_copies(matrices_ref, place_ref[0], buffer, sem)
    copy_piece, depth = piece_copies(matrices_ref, place_ref[0], buffer, piece_sem)
    for piece in range(rows // depth):
        copy_piece(jnp.int32(piece)).start()
    for term in range(1, min(SLOTS, count)):
        copy(jnp.int32(term)).start()
    out_ref[...] = jnp.zeros_like(out_ref)
    at = [order.index(member) for member in range(len(order))]

    def step_piece(piece, carry):
        copy_piece(piece).wait()
        block = buffer[0, pl.ds(pl.multiple_of(piece * depth, depth), depth), :]
        places = [pl.ds(pl.multiple_of(i * chunk, chunk), chunk) for i in (piece, len(order) - 1 - piece)]
        vecs = [jnp.concatenate([ref[place, :] for place in places], axis=0) for ref in (high_ref, low_ref)]
        out_ref[...] += product(halves(block), vecs, ((0,), (0,))) * weights_ref[0:1, :]
        return carry

    lax.fori_loop(0, rows // depth, step_piece, 0)

    def step(term):
        vecs = [
            jnp.concatenate([ref[i * chunk : (i + 1) * chunk, :] for i in at], axis=0) for ref in (high_ref, low_ref)
        ]
        terms = product(halves(buffer[lax.rem(term, SLOTS)]), vecs, ((0,), (0,)))
        out_ref[...] += terms * weights_ref[pl.ds(term, 1), :]

    each_matrix(1, count, copy, step)


VMEM = pl.BlockSpec(memory_space=pltpu.VMEM)
SMEM = pl.BlockSpec(memory_space=pltpu.SMEM)
ANY = pl.BlockSpec(memory_space=pl.ANY)


def cost(count, rows, width, trip):
    return pl.CostEstimate(
        flops=6 * count * rows * width * trip, bytes_accessed=4 * count * rows * width, transcendentals=0
    )


def right_terms(order, matrices, vecs, weights, place, total=None):
    count, rows, _ = matrices.shape
    width, trip = vecs.shape
    return pl.pallas_call(
        functools.partial(right_kernel, order, total is not None),
        out_shape=jax.ShapeDtypeStruct((rows, trip), jnp.float32),
        in_specs=[SMEM, ANY, VMEM, VMEM] + ([VMEM] if total is not None else []),
        out_specs=VMEM,
        scratch_shapes=[
            pltpu.VMEM((count, width, trip), jnp.bfloat16),
            pltpu.VMEM((count, width, trip), jnp.bfloat16),
            pltpu.VMEM((SLOTS, rows, width), jnp.float32),
            pltpu.SemaphoreType.DMA((SLOTS,)),
            pltpu.SemaphoreType.DMA((len(order) // 2,)),
        ],
        compiler_params=pltpu.CompilerParams(vmem_limit_bytes=VMEM_LIMIT),
        cost_estimate=cost(count, rows, width, trip),
        name="right_terms",
    )(jnp.reshape(place, (1,)), matrices, vecs, weights, *([total] if total is not None else []))


def left_terms(order, matrices, vecs, weights, place, width):
    count, rows, _ = matrices.shape
    trip = vecs[0].shape[1]
    return pl.pallas_call(
        functools.partial(left_kernel, order),
        out_shape=jax.ShapeDtypeStruct((width, trip), jnp.float32),
        in_specs=[SMEM, ANY, VMEM, VMEM, VMEM],
        out_specs=VMEM,
        scratch_shapes=[
            pltpu.VMEM((SLOTS, rows, width), jnp.float32),
            pltpu.SemaphoreType.DMA((SLOTS,)),
            pltpu.SemaphoreType.DMA((len(order) // 2,)),
        ],
        compiler_params=pltpu.CompilerParams(vmem_limit_bytes=VMEM_LIMIT),
        cost_estimate=cost(count, rows, width, trip),
        name="left_terms",
    )(jnp.reshape(place, (1,)), matrices, *vecs, weights)


def exchange(values, axis, size, bit):
    return lax.ppermute(values, axis, [(i, i ^ bit) for i in range(size)])


def squares(values):
    return jnp.sum(values * values, axis=0)


def body(n_row, n_col, coefficients, lambdas, right_vecs, left_vecs):
    order = ring_order(n_col)
    weights = chebyshev(lambdas, coefficients.shape[0])
    share = right_vecs.shape[0]
    pair = 2 * share
    left_rows = lax.all_gather(left_vecs, "col", axis=0, tiled=True, axis_index_groups=[order])

    left_high = lax.reduce_precision(left_rows, 8, 7)
    left_halves = (left_high.astype(jnp.bfloat16), (left_rows - left_high).astype(jnp.bfloat16))

    row = lax.axis_index("row").astype(jnp.int32)
    core = lax.rem(row, 2)
    if n_row == 4 and pair % LANES == 0:
        here = row // 2
        there = 1 - here
        other = exchange(right_vecs, "row", n_row, 1)
        near_vecs = jnp.where(core == 0, jnp.concatenate([right_vecs, other]), jnp.concatenate([other, right_vecs]))
        far_vecs = exchange(near_vecs, "row", n_row, 2)
        right = right_terms(order, coefficients, near_vecs, weights, here)
        right = right_terms(order, coefficients, far_vecs, weights, there, right)
    else:
        right_cols = lax.all_gather(right_vecs, "row", axis=0, tiled=True)
        right = right_terms(order, coefficients, right_cols, weights, jnp.int32(0))
    right_resid = lax.psum_scatter(right, "col", scatter_dimension=0, tiled=True, axis_index_groups=[order])
    right_squares = squares(right_resid)

    if n_row == 4 and pair % LANES == 0:
        sent = left_terms(order, coefficients, left_halves, weights, there, pair)
        came = exchange(sent, "row", n_row, 2)
        kept = left_terms(order, coefficients, left_halves, weights, here, pair)

        def part(values, which):
            return lax.dynamic_slice_in_dim(values, which * share, share, 0)

        other = part(kept, 1 - core) + part(came, 1 - core)
        last, right_squares = lax.optimization_barrier((exchange(other, "row", n_row, 1), right_squares))
        left_resid = part(kept, core) + part(came, core) + last
    else:
        left = left_terms(order, coefficients, left_halves, weights, jnp.int32(0), n_row * share)
        left_resid = lax.psum_scatter(left, "row", scatter_dimension=0, tiled=True)

    sums = jnp.stack([right_squares, squares(left_resid)])
    devices = n_row * n_col
    copies = jnp.broadcast_to(sums[None], (devices,) + sums.shape)
    parts = lax.all_to_all(copies, ("row", "col"), split_axis=0, concat_axis=0, tiled=True)
    rows = coefficients.shape[1] * n_row
    root_mean = jnp.sqrt(jnp.sum(parts, axis=0) / rows + epsilon)
    return (right_resid, left_resid, root_mean)


def solution(mesh):
    return jax.shard_map(
        functools.partial(body, mesh.shape["row"], mesh.shape["col"]),
        mesh=mesh,
        in_specs=(P(None, "row", "col"), P(), P(("col", "row"), None), P(("row", "col"), None)),
        out_specs=(P(("row", "col"), None), P(("col", "row"), None), P()),
        check_vma=False,
    )
```
